512 devices in a mesh: pair: 8 (over z_hi, y), blk: 64 (over z_lo, x, core).
Axes of the slice: x: 4, y: 4, z: 16 (z_hi: 2, z_lo: 8; z = z_hi * 8 + z_lo), core: 2. Of those that a mesh axis runs over, the one named last changes fastest.
Arguments:
- amps: bfloat16 [8192, 80200], P(('blk', 'pair')), may hold values from -6 to 6
- ints: bfloat16 [1024, 80200], P('blk', 'pair'), may hold values from -0.015625 to 0.015625
- block_of: int32 [64], replicated, may hold values from 0 to 63, each once
- pair_rows: int32 [8192, 2], P(('blk', 'pair')), may hold values from 0 to 119
- occ_energy: float32 [120], replicated, may hold values from -2 to -0.5
- vir_pair_energy: float32 [1024], replicated, may hold values from 1 to 6
Outputs:
- new_amps: float32 [8192, 1024], P(('blk', 'pair'))
The draws below stay inside these ranges and needn't reach their ends.
Inputs may be any that keep to these rules, and one draw needn't show every extreme that they name: `block_of`: each of 0 to 63 once.
All inputs are finite; a program needn't handle non-finite values.
Results may differ from the reference program's by a relative error of at most 0.0003.
Values may be sent and summed in bfloat16 or wider, within the bound.
A program may use at most 128 MiB of HBM per device.

```python
import jax
import jax.numpy as jnp
from jax import lax

NO = 120
NV = 400
CD = 80200
AB_DEV = 16
BLOCKS = 64
OP = 8192
AB = 1024


def with_ends(array, key, least, top_value):
    shape = array.shape
    place = [jax.random.randint(jax.random.fold_in(key, axis), (), 0, shape[axis]) for axis in range(len(shape))]
    array = array.at[tuple(place)].set(least)
    longest = shape.index(max(shape))
    place[longest] = (place[longest] + 1) % shape[longest]
    return array.at[tuple(place)].set(top_value)


def level_of(rng, shape, shards, smallest, top_value):
    gain, own = 1.0, jax.random.fold_in(rng, 6)
    for axis_at, parts in shards:
        heights = jnp.exp(jax.random.uniform(jax.random.fold_in(own, axis_at), (parts,), jnp.float32, smallest / len(shards), top_value / len(shards)))
        gain = gain * jnp.repeat(heights, shape[axis_at] // parts).reshape([-1 if axis == axis_at else 1 for axis in range(len(shape))])
    return gain


def noise(key, dims, spread, most, pieces=(), kind=jnp.bfloat16):
    entries = jax.random.normal(key, dims, jnp.float32) * spread
    if len(pieces) > 0:
        entries = level_of(key, dims, pieces, -0.22, 0.18) * entries
    return jnp.clip(entries, min=-most, max=most).astype(kind)


def setup_inputs(seed: int = 0) -> dict:
    key_of = jax.random.split(jax.random.key(seed), 7)
    return {
        "amps": noise(key_of[0], (OP, CD), 1.0, 6.0, ((0, 512),)),
        "ints": noise(key_of[1], (AB, CD), (2 * CD) ** -0.5, 0.015625, ((0, 64), (1, 8))),
        "block_of": jax.random.permutation(key_of[2], BLOCKS).astype(jnp.int32),
        "pair_rows": with_ends(jax.random.randint(key_of[3], (OP, 2), 0, NO), jax.random.fold_in(key_of[3], 1), 0, NO - 1).astype(jnp.int32),
        "occ_energy": jnp.clip(jax.random.uniform(key_of[4], (NO,), jnp.float32, -2.0, -0.5), -2.0, -0.5),
        "vir_pair_energy": jnp.clip(jax.random.uniform(key_of[5], (AB,), jnp.float32, 1.0, 6.0), 1.0, 6.0),
    }


def reference(amps, ints, block_of, pair_rows, occ_energy, vir_pair_energy):
    column = jnp.arange(ints.shape[1], dtype=jnp.int32)[None, :]
    weight = jnp.where(column < NV, 1.0, 2.0).astype(jnp.bfloat16)
    weighted_ints = ints * weight
    ladder_raw = lax.dot_general(amps, weighted_ints, (((1,), (1,)), ((), ())), preferred_element_type=jnp.float32)
    grouped = ladder_raw.reshape(OP, BLOCKS, AB_DEV)
    ladder = jnp.zeros_like(grouped).at[:, block_of].set(grouped).reshape(OP, AB)
    occupied = occ_energy[pair_rows[:, 0]] + occ_energy[pair_rows[:, 1]]
    denominator = vir_pair_energy[None, :] - occupied[:, None]
    return ladder / denominator
```

```python
import functools

import jax
import jax.numpy as jnp
from jax import lax
from jax.experimental import pallas as pl
from jax.experimental.pallas import tpu as pltpu
from jax.sharding import PartitionSpec as P

NV = 400
CD = 80200
RANGE = 10025
LANES = 128
WIDE = 10240
PIECE = 1280
LAST_TILE = 547
TAIL = LAST_TILE * LANES + WIDE - PIECE
Z, ZLO, Y, X = 16, 8, 4, 4
PLANE = 32
ROWS = 16
MESH = pl.DeviceIdType.MESH
F32, BF16 = jnp.float32, jnp.bfloat16

ORDER = (4, 3, 5, 2, 6, 1, 7, 0)
GROUPS = ((0, 1), (1, 3), (3, 5), (5, 7), (7, 8))
NT = (((1,), (1,)), ((), ()))


def first_tile(p):
    return jnp.minimum((RANGE * p) // LANES, LAST_TILE)


def kernel(
    amps, tail, wide, block_of, rows, occ, vir, out,
    a_buf, g_buf, prep, part, sib, got, acc, den_buf,
    i_send, i_recv, i_own, a_send, a_recv, a_own, r_send, r_recv, s_send, s_recv, q_send, q_recv,
):
    pair, blk = lax.axis_index("pair"), lax.axis_index("blk")
    zh, y = pair // Y, pair % Y
    zl, x, c = blk // (X * 2), (blk // 2) % X, blk % 2
    z = zh * ZLO + zl

    def device(z_at, y_at, x_at, c_at):
        return ((z_at // ZLO) * Y + y_at, ((z_at % ZLO) * X + x_at) * 2 + c_at)

    up, down = device((z + 1) % Z, y, x, c), device((z + Z - 1) % Z, y, x, c)
    twin = device(z, y, x, 1 - c)

    def peer(k):
        dc, dy, dx = k // 16, (k // 4) % 4, k % 4
        return (y + dy) % Y, (x + dx) % X, (c + dc) % 2

    def back(k):
        dc, dy, dx = k // 16, (k // 4) % 4, k % 4
        return (y + Y - dy) % Y, (x + X - dx) % X, (c + dc) % 2

    barrier = pltpu.get_barrier_semaphore()

    def greet(k, carry):
        pl.semaphore_signal(barrier, inc=1, device_id=device(z, *peer(k)), device_id_type=MESH)
        return carry

    lax.fori_loop(1, PLANE, greet, 0)
    for where in (up, down):
        pl.semaphore_signal(barrier, inc=1, device_id=where, device_id_type=MESH)

    offset = RANGE * pair - first_tile(pair) * LANES
    shift, skip = offset % LANES, offset // LANES
    lane = lax.broadcasted_iota(jnp.int32, (ROWS, LANES), 1)
    keep = lane >= shift

    def align(i, before):
        for j in range(8):
            tile = i * 8 + j
            at = pl.ds(pl.multiple_of(tile * LANES, LANES), LANES)
            now = pltpu.roll(wide[:, at].astype(F32), shift, 1)
            to = pl.multiple_of(((tile + skip) % 80) * LANES, LANES)
            prep[:, pl.ds(to, LANES)] = jnp.where(keep, now, before).astype(BF16)
            before = now
        return before

    lax.fori_loop(0, 10, align, jnp.zeros((ROWS, LANES), F32))

    pl.semaphore_wait(barrier, PLANE - 1 + 2)

    def ints_copy(k):
        x_to, c_to = (x + k // 2) % X, (c + k % 2) % 2
        src = prep.at[:, pl.ds(pl.multiple_of((x_to * 2 + c_to) * PIECE, LANES), PIECE)]
        return src, g_buf.at[0, x * 2 + c], device(z, y, x_to, c_to)

    src, dst, _ = ints_copy(0)
    own_ints = pltpu.make_async_copy(src, dst, i_own)
    own_ints.start()

    def send_ints(k, carry):
        src, dst, where = ints_copy(k)
        pltpu.make_async_remote_copy(src, dst, i_send, i_recv, device_id=where, device_id_type=MESH).start()
        return carry

    lax.fori_loop(1, 8, send_ints, 0)

    def amps_at(half, y_to, x_to, c_to):
        q = x_to * 2 + c_to
        p = half * Y + y_to
        start = pl.multiple_of(first_tile(p) * LANES + q * PIECE, LANES)
        return start, jnp.logical_and(p == 7, q == 7)

    def send_amps(k, carry):
        y_to, x_to, c_to = peer(k)
        for half in range(2):
            start, last = amps_at(half, y_to, x_to, c_to)
            dst = a_buf.at[half, pl.ds(pl.multiple_of(k * ROWS, ROWS), ROWS)]

            @pl.when(jnp.logical_not(last))
            def _():
                pltpu.make_async_remote_copy(
                    amps.at[:, pl.ds(start, PIECE)], dst, a_send, a_recv,
                    device_id=device(z, y_to, x_to, c_to), device_id_type=MESH,
                ).start()

            @pl.when(last)
            def _():
                pltpu.make_async_remote_copy(
                    tail, dst, a_send, a_recv,
                    device_id=device(z, y_to, x_to, c_to), device_id_type=MESH,
                ).start()

        return carry

    lax.fori_loop(1, PLANE, send_amps, 0)
    for half in range(2):
        start, last = amps_at(half, y, x, c)
        dst = a_buf.at[half, 0:ROWS]

        @pl.when(jnp.logical_not(last))
        def _():
            pltpu.make_async_copy(amps.at[:, pl.ds(start, PIECE)], dst, a_own.at[half]).start()

        @pl.when(last)
        def _():
            pltpu.make_async_copy(tail, dst, a_own.at[half]).start()

    occ_lane = lax.broadcasted_iota(jnp.int32, (ROWS, occ.shape[1]), 1)
    e_i = jnp.sum(jnp.where(rows[:, 0:1] == occ_lane, occ[...], 0.0), axis=1, keepdims=True)
    e_j = jnp.sum(jnp.where(rows[:, 1:2] == occ_lane, occ[...], 0.0), axis=1, keepdims=True)
    den_buf[...] = vir[...] - (e_i + e_j)
    acc[...] = jnp.zeros_like(acc)

    own_ints.wait()
    seven = g_buf.at[0, 0:7]
    pltpu.make_async_copy(seven, seven, i_recv).wait()

    def hop(m_from, m_to, part_at, where):
        sl = pl.ds(part_at * 4, 4)
        return pltpu.make_async_remote_copy(
            g_buf.at[m_from, sl], g_buf.at[m_to, sl], r_send.at[m_to, part_at], r_recv.at[m_to, part_at],
            device_id=where, device_id_type=MESH,
        )

    def forward(step):
        for part_at in range(2):
            ways = [(step, (step - 1) % Z, up), (Z - step, (Z - step + 1) % Z, down)]
            if step == 8:
                ways = [ways[part_at]]
            for m_to, m_from, where in ways:
                if step > 1:
                    hop(m_from, m_from, part_at, where).wait_recv()
                hop(m_from, m_to, part_at, where).start()

    def compute(group):
        lo, hi = GROUPS[group]
        for o in range(lo, hi):
            b = ORDER[o]
            half = ((z + Z - b) % Z) // ZLO
            low = g_buf[b].reshape(LANES, PIECE)
            high = g_buf[b + 8].reshape(LANES, PIECE)
            part[o] = lax.dot_general(a_buf[half], low, NT, preferred_element_type=F32) + lax.dot_general(
                a_buf[1 - half], high, NT, preferred_element_type=F32
            )
        twin_copy(group).start()

    def twin_copy(group):
        lo, hi = GROUPS[group]
        return pltpu.make_async_remote_copy(
            part.at[lo:hi, 256:512], sib.at[lo:hi], s_send.at[group], s_recv.at[group],
            device_id=twin, device_id_type=MESH,
        )

    def spread(group):
        lo, hi = GROUPS[group]
        twin_copy(group).wait_recv()
        for o in range(lo, hi):
            part[o, 0:256] += sib[o]

        def send_sum(k, carry):
            sl = pl.ds(pl.multiple_of(k * ROWS, ROWS), ROWS)
            pltpu.make_async_remote_copy(
                part.at[lo:hi, sl], got.at[lo:hi, sl], q_send.at[group], q_recv.at[group],
                device_id=device(z, *back(k)), device_id_type=MESH,
            ).start()
            return carry

        lax.fori_loop(1, 16, send_sum, 0)

    def finish(group):
        lo, hi = GROUPS[group]
        arrived = got.at[lo:hi, ROWS:256]
        pltpu.make_async_copy(arrived, arrived, q_recv.at[group]).wait()
        column = lax.broadcasted_iota(jnp.int32, (1, LANES), 1)
        for o in range(lo, hi):
            total = part[o, 0:ROWS]
            for k in range(1, 16):
                total = total + got[o, k * ROWS : (k + 1) * ROWS]
            top = total.astype(BF16)
            rest = total - top.astype(F32)
            mid = rest.astype(BF16)
            low = (rest - mid.astype(F32)).astype(BF16)
            block = (zl + ZLO - ORDER[o]) % ZLO
            held = block_of[pl.ds(block, 1), :]
            goes = jnp.zeros((1, LANES), jnp.int32)
            for j in range(8):
                goes = jnp.where(column // 16 == j, held[:, j : j + 1], goes)
            goes = goes * 16 + column % 16
            place = lax.broadcasted_iota(jnp.int32, (1024, LANES), 0)
            moves = jnp.where(place == goes, 1.0, 0.0).astype(BF16)
            moved = lax.dot_general(
                jnp.concatenate([top, mid, low], axis=0), moves, NT, preferred_element_type=F32
            )
            acc[...] += moved[0:16] + moved[16:32] + moved[32:48]

    for step in range(1, 6):
        forward(step)
    pltpu.make_async_copy(amps.at[:, 0:PIECE], a_buf.at[0, 0:ROWS], a_own.at[0]).wait()
    pltpu.make_async_copy(amps.at[:, 0:PIECE], a_buf.at[1, 0:ROWS], a_own.at[1]).wait()
    others = a_buf.at[:, ROWS:512]
    pltpu.make_async_copy(others, others, a_recv).wait()
    compute(0)
    forward(6)
    spread(0)
    compute(1)
    forward(7)
    spread(1)
    compute(2)
    forward(8)
    spread(2)
    hop(7, 7, 1, up).wait_recv()
    hop(9, 9, 0, down).wait_recv()
    compute(3)
    finish(0)
    finish(1)
    spread(3)
    hop(8, 8, 0, up).wait_recv()
    hop(8, 8, 1, down).wait_recv()
    compute(4)
    finish(2)
    spread(4)
    finish(3)
    finish(4)
    out[...] = acc[...] / den_buf[...]

    pltpu.make_async_copy(seven, seven, i_send).wait()
    pltpu.make_async_copy(others, others, a_send).wait()
    for step in range(1, 9):
        for part_at in range(2):
            if step < 8 or part_at == 0:
                hop(step, step, part_at, up).wait_send()
            if step < 8 or part_at == 1:
                hop(Z - step, Z - step, part_at, down).wait_send()
    for group in range(5):
        lo, hi = GROUPS[group]
        twin_copy(group).wait_send()
        arrived = got.at[lo:hi, ROWS:256]
        pltpu.make_async_copy(arrived, arrived, q_send.at[group]).wait()


def per_device(amps, ints, block_of, pair_rows, occ_energy, vir_pair_energy):
    column = lax.axis_index("pair") * RANGE + lax.broadcasted_iota(jnp.int32, (1, RANGE), 1)
    weighted = ints * jnp.where(column < NV, 1.0, 2.0).astype(BF16)
    wide = jnp.pad(weighted, ((0, 0), (0, WIDE - RANGE)))
    tail = jnp.pad(amps[:, TAIL:], ((0, 0), (0, TAIL + PIECE - CD)))
    vmem = pl.BlockSpec(memory_space=pltpu.VMEM)
    hbm = pl.BlockSpec(memory_space=pl.ANY)
    dma = pltpu.SemaphoreType.DMA
    return pl.pallas_call(
        kernel,
        out_shape=jax.ShapeDtypeStruct((ROWS, 1024), F32),
        in_specs=[hbm, vmem, vmem, vmem, vmem, vmem, vmem],
        out_specs=vmem,
        scratch_shapes=[
            pltpu.VMEM((2, 512, PIECE), BF16),
            pltpu.VMEM((Z, 8, ROWS, PIECE), BF16),
            pltpu.VMEM((ROWS, WIDE), BF16),
            pltpu.VMEM((8, 512, LANES), F32),
            pltpu.VMEM((8, 256, LANES), F32),
            pltpu.VMEM((8, 256, LANES), F32),
            pltpu.VMEM((ROWS, 1024), F32),
            pltpu.VMEM((ROWS, 1024), F32),
            dma, dma, dma, dma, dma, dma((2,)),
            dma((Z, 2)), dma((Z, 2)), dma((5,)), dma((5,)), dma((5,)), dma((5,)),
        ],
        compiler_params=pltpu.CompilerParams(
            collective_id=0, has_side_effects=True, vmem_limit_bytes=40 * 1024 * 1024
        ),
        cost_estimate=pl.CostEstimate(flops=2700000000, bytes_accessed=4000000, transcendentals=0),
    )(
        amps, tail, wide, block_of.reshape(8, 8), pair_rows,
        occ_energy.reshape(1, -1), vir_pair_energy.reshape(1, -1),
    )


def solution(mesh):
    placed = (P(("blk", "pair"), None), P("blk", "pair"), P(), P(("blk", "pair"), None), P(), P())
    return jax.shard_map(
        per_device, mesh=mesh, in_specs=placed, out_specs=P(("blk", "pair"), None), check_vma=False
    )
```

```python
import functools

import jax
import jax.numpy as jnp
from jax import lax
from jax.experimental import pallas as pl
from jax.experimental.pallas import tpu as pltpu
from jax.sharding import PartitionSpec as P

NV = 400
CD = 80200
RANGE = 10025
LANES = 128
WIDE = 10240
PIECE = 1280
LAST_TILE = 547
TAIL = LAST_TILE * LANES + WIDE - PIECE
Z, ZLO, Y, X = 16, 8, 4, 4
PLANE = 32
BLOCKS = 64
ROWS = 16
MESH = pl.DeviceIdType.MESH
F32, BF16 = jnp.float32, jnp.bfloat16

ORDER = (4, 3, 5, 2, 6, 1, 7, 0)
GROUPS = ((0, 1), (1, 3), (3, 5), (5, 7), (7, 8))
NT = (((1,), (1,)), ((), ()))


def first_tile(p):
    return jnp.minimum((RANGE * p) // LANES, LAST_TILE)


def kernel(
    amps, ints, block_of, rows, occ, vir, out,
    a_buf, g_buf, held, last, tail, prep, part, sib, got, acc, den_buf, in_sem,
    i_send, i_recv, i_own, a_send, a_recv, a_own, r_send, r_recv, s_send, s_recv, q_send, q_recv,
):
    pair, blk = lax.axis_index("pair"), lax.axis_index("blk")
    zh, y = pair // Y, pair % Y
    zl, x, c = blk // (X * 2), (blk // 2) % X, blk % 2
    z = zh * ZLO + zl

    def device(z_at, y_at, x_at, c_at):
        return ((z_at // ZLO) * Y + y_at, ((z_at % ZLO) * X + x_at) * 2 + c_at)

    up, down = device((z + 1) % Z, y, x, c), device((z + Z - 1) % Z, y, x, c)
    twin = device(z, y, x, 1 - c)

    def peer(k):
        dc, dy, dx = k // 16, (k // 4) % 4, k % 4
        return (y + dy) % Y, (x + dx) % X, (c + dc) % 2

    def back(k):
        dc, dy, dx = k // 16, (k // 4) % 4, k % 4
        return (y + Y - dy) % Y, (x + X - dx) % X, (c + dc) % 2

    get_ints = pltpu.make_async_copy(ints, held, in_sem.at[0])
    get_ints.start()
    get_tail = pltpu.make_async_copy(amps.at[:, TAIL:CD], last.at[:, :], in_sem.at[1])
    get_tail.start()

    barrier = pltpu.get_barrier_semaphore()

    def greet(k, carry):
        pl.semaphore_signal(barrier, inc=1, device_id=device(z, *peer(k)), device_id_type=MESH)
        return carry

    lax.fori_loop(1, PLANE, greet, 0)
    for where in (up, down):
        pl.semaphore_signal(barrier, inc=1, device_id=where, device_id_type=MESH)

    offset = RANGE * pair - first_tile(pair) * LANES
    shift, skip = offset % LANES, offset // LANES
    lane = lax.broadcasted_iota(jnp.int32, (ROWS, LANES), 1)
    keep = lane >= shift

    def put(tile, value, before):
        now = pltpu.roll(value, shift, 1)
        to = pl.multiple_of(((tile + skip) % 80) * LANES, LANES)
        prep[:, pl.ds(to, LANES)] = jnp.where(keep, now, before).astype(BF16)
        return now

    def align(i, before):
        for j in range(6):
            tile = i * 6 + j
            at = pl.ds(pl.multiple_of(tile * LANES, LANES), LANES)
            column = RANGE * pair + tile * LANES + lane
            weight = jnp.where(column < NV, 1.0, 2.0)
            before = put(tile, held[:, at].astype(F32) * weight, before)
        return before

    get_ints.wait()
    before = lax.fori_loop(0, 13, align, jnp.zeros((ROWS, LANES), F32))
    rest = held[:, 78 * LANES : RANGE].astype(F32) * 2.0
    rest = jnp.concatenate([rest, jnp.zeros((ROWS, 79 * LANES - RANGE), F32)], axis=1)
    before = put(78, rest, before)
    put(79, jnp.zeros((ROWS, LANES), F32), before)
    get_tail.wait()
    tail[:, 0 : PIECE - LANES] = last[:, 0 : PIECE - LANES]
    ending = last[:, PIECE - LANES :]
    tail[:, PIECE - LANES :] = jnp.concatenate([ending, jnp.zeros((ROWS, TAIL + PIECE - CD), BF16)], axis=1)

    pl.semaphore_wait(barrier, PLANE - 1 + 2)

    def ints_copy(k):
        x_to, c_to = (x + k // 2) % X, (c + k % 2) % 2
        src = prep.at[:, pl.ds(pl.multiple_of((x_to * 2 + c_to) * PIECE, LANES), PIECE)]
        return src, g_buf.at[0, x * 2 + c], device(z, y, x_to, c_to)

    src, dst, _ = ints_copy(0)
    own_ints = pltpu.make_async_copy(src, dst, i_own)
    own_ints.start()

    def send_ints(k, carry):
        src, dst, where = ints_copy(k)
        pltpu.make_async_remote_copy(src, dst, i_send, i_recv, device_id=where, device_id_type=MESH).start()
        return carry

    lax.fori_loop(1, 8, send_ints, 0)

    def amps_at(half, y_to, x_to, c_to):
        q = x_to * 2 + c_to
        p = half * Y + y_to
        start = pl.multiple_of(first_tile(p) * LANES + q * PIECE, LANES)
        return start, jnp.logical_and(p == 7, q == 7)

    def send_amps(k, carry):
        y_to, x_to, c_to = peer(k)
        for half in range(2):
            start, ends = amps_at(half, y_to, x_to, c_to)
            dst = a_buf.at[half, pl.ds(pl.multiple_of(k * ROWS, ROWS), ROWS)]

            @pl.when(jnp.logical_not(ends))
            def _():
                pltpu.make_async_remote_copy(
                    amps.at[:, pl.ds(start, PIECE)], dst, a_send, a_recv,
                    device_id=device(z, y_to, x_to, c_to), device_id_type=MESH,
                ).start()

            @pl.when(ends)
            def _():
                pltpu.make_async_remote_copy(
                    tail, dst, a_send, a_recv,
                    device_id=device(z, y_to, x_to, c_to), device_id_type=MESH,
                ).start()

        return carry

    lax.fori_loop(1, PLANE, send_amps, 0)
    for half in range(2):
        start, ends = amps_at(half, y, x, c)
        dst = a_buf.at[half, 0:ROWS]

        @pl.when(jnp.logical_not(ends))
        def _():
            pltpu.make_async_copy(amps.at[:, pl.ds(start, PIECE)], dst, a_own.at[half]).start()

        @pl.when(ends)
        def _():
            pltpu.make_async_copy(tail, dst, a_own.at[half]).start()

    occ_lane = lax.broadcasted_iota(jnp.int32, (ROWS, occ.shape[1]), 1)
    square = (ROWS, ROWS)
    diagonal = lax.broadcasted_iota(jnp.int32, square, 0) == lax.broadcasted_iota(jnp.int32, square, 1)

    def energy(which):
        orbital = jnp.where(diagonal, rows[which : which + 1, :].astype(F32), 0.0)
        orbital = jnp.sum(orbital, axis=1, keepdims=True).astype(jnp.int32)
        return jnp.sum(jnp.where(orbital == occ_lane, occ[...], 0.0), axis=1, keepdims=True)

    den_buf[...] = vir[...] - (energy(0) + energy(1))
    acc[...] = jnp.zeros_like(acc)

    own_ints.wait()
    seven = g_buf.at[0, 0:7]
    pltpu.make_async_copy(seven, seven, i_recv).wait()

    def hop(m_from, m_to, part_at, where):
        sl = pl.ds(part_at * 4, 4)
        return pltpu.make_async_remote_copy(
            g_buf.at[m_from, sl], g_buf.at[m_to, sl], r_send.at[m_to, part_at], r_recv.at[m_to, part_at],
            device_id=where, device_id_type=MESH,
        )

    def forward(step):
        for part_at in range(2):
            ways = [(step, (step - 1) % Z, up), (Z - step, (Z - step + 1) % Z, down)]
            if step == 8:
                ways = [ways[part_at]]
            for m_to, m_from, where in ways:
                if step > 1:
                    hop(m_from, m_from, part_at, where).wait_recv()
                hop(m_from, m_to, part_at, where).start()

    def compute(group):
        lo, hi = GROUPS[group]
        for o in range(lo, hi):
            b = ORDER[o]
            half = ((z + Z - b) % Z) // ZLO
            low = g_buf[b].reshape(LANES, PIECE)
            high = g_buf[b + 8].reshape(LANES, PIECE)
            part[o] = lax.dot_general(a_buf[half], low, NT, preferred_element_type=F32) + lax.dot_general(
                a_buf[1 - half], high, NT, preferred_element_type=F32
            )
        twin_copy(group).start()

    def twin_copy(group):
        lo, hi = GROUPS[group]
        return pltpu.make_async_remote_copy(
            part.at[lo:hi, 256:512], sib.at[lo:hi], s_send.at[group], s_recv.at[group],
            device_id=twin, device_id_type=MESH,
        )

    def spread(group):
        lo, hi = GROUPS[group]
        twin_copy(group).wait_recv()
        for o in range(lo, hi):
            part[o, 0:256] += sib[o]

        def send_sum(k, carry):
            sl = pl.ds(pl.multiple_of(k * ROWS, ROWS), ROWS)
            pltpu.make_async_remote_copy(
                part.at[lo:hi, sl], got.at[lo:hi, sl], q_send.at[group], q_recv.at[group],
                device_id=device(z, *back(k)), device_id_type=MESH,
            ).start()
            return carry

        lax.fori_loop(1, 16, send_sum, 0)

    def finish(group):
        lo, hi = GROUPS[group]
        arrived = got.at[lo:hi, ROWS:256]
        pltpu.make_async_copy(arrived, arrived, q_recv.at[group]).wait()
        column = lax.broadcasted_iota(jnp.int32, (1, LANES), 1)
        for o in range(lo, hi):
            total = part[o, 0:ROWS]
            for k in range(1, 16):
                total = total + got[o, k * ROWS : (k + 1) * ROWS]
            top = total.astype(BF16)
            rest = total - top.astype(F32)
            mid = rest.astype(BF16)
            low = (rest - mid.astype(F32)).astype(BF16)
            block = (zl + ZLO - ORDER[o]) % ZLO
            rows_at = lax.broadcasted_iota(jnp.int32, (BLOCKS, LANES), 0)
            pick = rows_at == block * 8 + lax.broadcasted_iota(jnp.int32, (BLOCKS, LANES), 1) // 16
            goes = lax.dot_general(
                block_of[...].astype(F32).astype(BF16), jnp.where(pick, 1.0, 0.0).astype(BF16),
                (((1,), (0,)), ((), ())), preferred_element_type=F32,
            )
            goes = goes.astype(jnp.int32) * 16 + column % 16
            place = lax.broadcasted_iota(jnp.int32, (1024, LANES), 0)
            moves = jnp.where(place == goes, 1.0, 0.0).astype(BF16)
            moved = lax.dot_general(
                jnp.concatenate([top, mid, low], axis=0), moves, NT, preferred_element_type=F32
            )
            acc[...] += moved[0:16] + moved[16:32] + moved[32:48]

    for step in range(1, 6):
        forward(step)
    pltpu.make_async_copy(amps.at[:, 0:PIECE], a_buf.at[0, 0:ROWS], a_own.at[0]).wait()
    pltpu.make_async_copy(amps.at[:, 0:PIECE], a_buf.at[1, 0:ROWS], a_own.at[1]).wait()
    others = a_buf.at[:, ROWS:512]
    pltpu.make_async_copy(others, others, a_recv).wait()
    compute(0)
    forward(6)
    spread(0)
    compute(1)
    forward(7)
    spread(1)
    compute(2)
    forward(8)
    spread(2)
    hop(7, 7, 1, up).wait_recv()
    hop(9, 9, 0, down).wait_recv()
    compute(3)
    finish(0)
    finish(1)
    spread(3)
    hop(8, 8, 0, up).wait_recv()
    hop(8, 8, 1, down).wait_recv()
    compute(4)
    finish(2)
    spread(4)
    finish(3)
    finish(4)
    out[...] = acc[...] / den_buf[...]

    pltpu.make_async_copy(seven, seven, i_send).wait()
    pltpu.make_async_copy(others, others, a_send).wait()
    for step in range(1, 9):
        for part_at in range(2):
            if step < 8 or part_at == 0:
                hop(step, step, part_at, up).wait_send()
            if step < 8 or part_at == 1:
                hop(Z - step, Z - step, part_at, down).wait_send()
    for group in range(5):
        lo, hi = GROUPS[group]
        twin_copy(group).wait_send()
        arrived = got.at[lo:hi, ROWS:256]
        pltpu.make_async_copy(arrived, arrived, q_send.at[group]).wait()


def per_device(amps, ints, block_of, pair_rows, occ_energy, vir_pair_energy):
    vmem = pl.BlockSpec(memory_space=pltpu.VMEM)
    hbm = pl.BlockSpec(memory_space=pl.ANY)
    dma = pltpu.SemaphoreType.DMA
    return pl.pallas_call(
        kernel,
        out_shape=jax.ShapeDtypeStruct((ROWS, 1024), F32),
        in_specs=[hbm, hbm, vmem, vmem, vmem, vmem],
        out_specs=vmem,
        scratch_shapes=[
            pltpu.VMEM((2, 512, PIECE), BF16),
            pltpu.VMEM((Z, 8, ROWS, PIECE), BF16),
            pltpu.VMEM((ROWS, RANGE), BF16),
            pltpu.VMEM((ROWS, CD - TAIL), BF16),
            pltpu.VMEM((ROWS, PIECE), BF16),
            pltpu.VMEM((ROWS, WIDE), BF16),
            pltpu.VMEM((8, 512, LANES), F32),
            pltpu.VMEM((8, 256, LANES), F32),
            pltpu.VMEM((8, 256, LANES), F32),
            pltpu.VMEM((ROWS, 1024), F32),
            pltpu.VMEM((ROWS, 1024), F32),
            dma((2,)), dma, dma, dma, dma, dma, dma((2,)),
            dma((Z, 2)), dma((Z, 2)), dma((5,)), dma((5,)), dma((5,)), dma((5,)),
        ],
        compiler_params=pltpu.CompilerParams(
            collective_id=0, has_side_effects=True, vmem_limit_bytes=56 * 1024 * 1024
        ),
        cost_estimate=pl.CostEstimate(flops=2700000000, bytes_accessed=4000000, transcendentals=0),
    )(
        amps, ints, block_of.reshape(1, -1), pair_rows.T,
        occ_energy.reshape(1, -1), vir_pair_energy.reshape(1, -1),
    )


def solution(mesh):
    placed = (P(("blk", "pair"), None), P("blk", "pair"), P(), P(("blk", "pair"), None), P(), P())
    return jax.shard_map(
        per_device, mesh=mesh, in_specs=placed, out_specs=P(("blk", "pair"), None), check_vma=False
    )
```

```python
import functools

import jax
import jax.numpy as jnp
from jax import lax
from jax.experimental import pallas as pl
from jax.experimental.pallas import tpu as pltpu
from jax.sharding import PartitionSpec as P

NV = 400
CD = 80200
RANGE = 10025
LANES = 128
WIDE = 10240
PIECE = 1280
LAST_TILE = 547
TAIL = LAST_TILE * LANES + WIDE - PIECE
Z, ZLO, Y, X = 16, 8, 4, 4
PLANE = 32
BLOCKS = 64
ROWS = 16
MESH = pl.DeviceIdType.MESH
F32, BF16 = jnp.float32, jnp.bfloat16

ORDER = (4, 3, 5, 2, 6, 1, 7, 0)
GROUPS = ((0, 1), (1, 3), (3, 5), (5, 7), (7, 8))
FIRST = (0, 1, 2, 3, 4, 5, 14, 15)
NEAR = (0, 1, 3, 2)
NT = (((1,), (1,)), ((), ()))


def first_tile(p):
    return jnp.minimum(lax.div(RANGE * p, LANES), LAST_TILE)


def kernel(
    amps, ints, block_of, rows, occ, vir, out,
    a_buf, g_buf, held, last, tail, prep, part, sib, got, acc, den_buf, in_sem,
    i_send, i_recv, i_own, a_send, a_recv, a_own, r_send, r_recv, s_send, s_recv, q_send, q_recv,
):
    pair, blk = lax.axis_index("pair"), lax.axis_index("blk")
    zh, y = lax.div(pair, Y), lax.rem(pair, Y)
    zl, x, c = lax.div(blk, X * 2), lax.rem(lax.div(blk, 2), X), lax.rem(blk, 2)
    z = zh * ZLO + zl

    def plane(z_at):
        return lax.div(z_at, ZLO) * Y, lax.rem(z_at, ZLO) * (X * 2)

    row, column = plane(z)
    ys, xs = [lax.rem(y + d, Y) for d in range(Y)], [lax.rem(x + d, X) for d in range(X)]
    up, down = plane(lax.rem(z + 1, Z)), plane(lax.rem(z + Z - 1, Z))
    up, down = ((p + y, b + x * 2 + c) for p, b in (up, down))
    twin = (pair, column + x * 2 + 1 - c)

    def device(y_at, x_at, c_at):
        return (row + y_at, column + x_at * 2 + c_at)

    def peer(k):
        dc, dy, dx = lax.div(k, 16), lax.rem(lax.div(k, 4), 4), lax.rem(k, 4)
        return lax.rem(y + dy, Y), lax.rem(x + dx, X), lax.rem(c + dc, 2)

    get_ints = pltpu.make_async_copy(ints, held, in_sem.at[0])
    get_ints.start()
    get_tail = pltpu.make_async_copy(amps.at[:, TAIL:CD], last.at[:, :], in_sem.at[1])
    get_tail.start()

    barrier = pltpu.get_barrier_semaphore()

    def greet(k, carry):
        pl.semaphore_signal(barrier, inc=1, device_id=device(*peer(k)), device_id_type=MESH)
        return carry

    lax.fori_loop(1, PLANE, greet, 0)
    for where in (up, down):
        pl.semaphore_signal(barrier, inc=1, device_id=where, device_id_type=MESH)

    offset = RANGE * pair - first_tile(pair) * LANES
    shift, skip = lax.rem(offset, LANES), lax.div(offset, LANES)
    lane = lax.broadcasted_iota(jnp.int32, (ROWS, LANES), 1)
    keep = lane >= shift

    def put(tile, value, before):
        now = pltpu.roll(value, shift, 1)
        to = pl.multiple_of(lax.rem(tile + skip, 80) * LANES, LANES)
        prep[:, pl.ds(to, LANES)] = jnp.where(keep, now, before).astype(BF16)
        return now

    def align(i, before):
        for j in range(6):
            tile = i * 6 + j
            at = pl.ds(pl.multiple_of(tile * LANES, LANES), LANES)
            column = RANGE * pair + tile * LANES + lane
            weight = jnp.where(column < NV, 1.0, 2.0)
            before = put(tile, held[:, at].astype(F32) * weight, before)
        return before

    get_ints.wait()
    before = lax.fori_loop(0, 13, align, jnp.zeros((ROWS, LANES), F32))
    rest = held[:, 78 * LANES : RANGE].astype(F32) * 2.0
    rest = jnp.concatenate([rest, jnp.zeros((ROWS, 79 * LANES - RANGE), F32)], axis=1)
    before = put(78, rest, before)
    put(79, jnp.zeros((ROWS, LANES), F32), before)
    get_tail.wait()
    tail[:, 0 : PIECE - LANES] = last[:, 0 : PIECE - LANES]
    ending = last[:, PIECE - LANES :]
    tail[:, PIECE - LANES :] = jnp.concatenate([ending, jnp.zeros((ROWS, TAIL + PIECE - CD), BF16)], axis=1)

    pl.semaphore_wait(barrier, PLANE - 1 + 2)

    def ints_copy(x_to, c_to):
        src = prep.at[:, pl.ds(pl.multiple_of((x_to * 2 + c_to) * PIECE, LANES), PIECE)]
        return src, g_buf.at[0, x * 2 + c]

    def send_ints(e, x_to, c_to):
        src, dst = ints_copy(x_to, c_to)
        pltpu.make_async_remote_copy(
            src, dst, i_send, i_recv.at[e], device_id=device(y, x_to, c_to), device_id_type=MESH
        ).start()

    send_ints(0, x, 1 - c)

    def amps_at(half, y_to, x_to, c_to):
        q = x_to * 2 + c_to
        p = half * Y + y_to
        start = pl.multiple_of(first_tile(p) * LANES + q * PIECE, LANES)
        return start, jnp.logical_and(p == 7, q == 7)

    def send_amps(k, carry):
        y_to, x_to, c_to = peer(k)
        for half in range(2):
            start, ends = amps_at(half, y_to, x_to, c_to)
            dst = a_buf.at[half, pl.ds(pl.multiple_of(k * ROWS, ROWS), ROWS)]

            @pl.when(jnp.logical_not(ends))
            def _():
                pltpu.make_async_remote_copy(
                    amps.at[:, pl.ds(start, PIECE)], dst, a_send, a_recv,
                    device_id=device(y_to, x_to, c_to), device_id_type=MESH,
                ).start()

            @pl.when(ends)
            def _():
                pltpu.make_async_remote_copy(
                    tail, dst, a_send, a_recv,
                    device_id=device(y_to, x_to, c_to), device_id_type=MESH,
                ).start()

        return carry

    for half in range(2):
        start, ends = amps_at(half, y, x, c)
        dst = a_buf.at[half, 0:ROWS]

        @pl.when(jnp.logical_not(ends))
        def _():
            pltpu.make_async_copy(amps.at[:, pl.ds(start, PIECE)], dst, a_own.at[half]).start()

        @pl.when(ends)
        def _():
            pltpu.make_async_copy(tail, dst, a_own.at[half]).start()

    def hop(m_from, m_to, at, where):
        sl = pl.ds(xs[-NEAR[at] % X] * 2, 2)
        return pltpu.make_async_remote_copy(
            g_buf.at[m_from, sl], g_buf.at[m_to, sl], r_send, r_recv.at[m_to, at],
            device_id=where, device_id_type=MESH,
        )

    def forward(step, quarters=range(4)):
        for at in quarters:
            ways = [(step, (step - 1) % Z, up), (Z - step, (Z - step + 1) % Z, down)]
            if step == 8:
                ways = [ways[at // 2]]
            if step == 1 and at == 0:
                continue
            if step == 1:
                came = g_buf.at[0, 0:2]
                pltpu.make_async_copy(came, came, i_recv.at[NEAR[at]]).wait()
            for m_to, m_from, where in ways:
                if step > 1:
                    hop(m_from, m_from, at, where).wait_recv()
                hop(m_from, m_to, at, where).start()
            if step == 1:
                lax.fori_loop(at * 8, at * 8 + 8, send_amps, 0)

    def start_ring():
        mine = pltpu.make_async_copy(*ints_copy(x, c), i_own)
        came = g_buf.at[0, 0]
        for own in (True, False):
            at = x * 2 + c if own else x * 2 + 1 - c
            if not own:
                pltpu.make_async_copy(came, came, i_recv.at[0]).wait()
            for m_to, where in ((1, up), (Z - 1, down)):
                pltpu.make_async_remote_copy(
                    ints_copy(x, c)[0] if own else g_buf.at[0, at], g_buf.at[m_to, at],
                    r_send, r_recv.at[m_to, 0], device_id=where, device_id_type=MESH,
                ).start()
            if own:
                mine.start()
                for e in NEAR[1:]:
                    for c_to in (c, 1 - c):
                        send_ints(e, xs[e], c_to)
        lax.fori_loop(1, 8, send_amps, 0)
        return mine

    def multiply(*slots, lines=slice(0, 512)):
        for m in slots:
            o = ORDER.index(m % 8)
            half = lax.div(lax.rem(z + Z - m, Z), ZLO)
            product = lax.dot_general(
                a_buf[half, lines], g_buf[m].reshape(LANES, PIECE), NT, preferred_element_type=F32
            )
            part[o, lines] = product if m in FIRST else part[o, lines] + product

    def twin_copy(group):
        lo, hi = GROUPS[group]
        return pltpu.make_async_remote_copy(
            part.at[lo:hi, 256:512], sib.at[lo:hi], s_send, s_recv.at[group],
            device_id=twin, device_id_type=MESH,
        )

    def spread(group):
        lo, hi = GROUPS[group]
        twin_copy(group).wait_recv()
        for o in range(lo, hi):
            part[o, 0:256] += sib[o]

        for k in range(1, 16):
            sl = slice(k * ROWS, (k + 1) * ROWS)
            pltpu.make_async_remote_copy(
                part.at[lo:hi, sl], got.at[lo:hi, sl], q_send, q_recv.at[group],
                device_id=device(ys[-(k // 4) % Y], xs[-k % X], c), device_id_type=MESH,
            ).start()

    def finish(group):
        lo, hi = GROUPS[group]
        arrived = got.at[lo:hi, ROWS:256]
        pltpu.make_async_copy(arrived, arrived, q_recv.at[group]).wait()
        spot = lax.broadcasted_iota(jnp.int32, (1, LANES), 1)
        for o in range(lo, hi):
            total = part[o, 0:ROWS]
            for k in range(1, 16):
                total = total + got[o, k * ROWS : (k + 1) * ROWS]
            top = total.astype(BF16)
            rest = total - top.astype(F32)
            mid = rest.astype(BF16)
            low = (rest - mid.astype(F32)).astype(BF16)
            block = lax.rem(zl + ZLO - ORDER[o], ZLO)
            rows_at = lax.broadcasted_iota(jnp.int32, (BLOCKS, LANES), 0)
            pick = rows_at == block * 8 + lax.broadcasted_iota(jnp.int32, (BLOCKS, LANES), 1) // 16
            goes = lax.dot_general(
                block_of[...].astype(F32).astype(BF16), jnp.where(pick, 1.0, 0.0).astype(BF16),
                (((1,), (0,)), ((), ())), preferred_element_type=F32,
            )
            goes = goes.astype(jnp.int32) * 16 + spot % 16
            place = lax.broadcasted_iota(jnp.int32, (1024, LANES), 0)
            moves = jnp.where(place == goes, 1.0, 0.0).astype(BF16)
            moved = lax.dot_general(
                jnp.concatenate([top, mid, low], axis=0), moves, NT, preferred_element_type=F32
            )
            acc[...] += moved[0:16] + moved[16:32] + moved[32:48]

    own_ints = start_ring()
    forward(1)
    occ_lane = lax.broadcasted_iota(jnp.int32, (ROWS, occ.shape[1]), 1)
    square = (ROWS, ROWS)
    diagonal = lax.broadcasted_iota(jnp.int32, square, 0) == lax.broadcasted_iota(jnp.int32, square, 1)

    def energy(which):
        orbital = jnp.where(diagonal, rows[which : which + 1, :].astype(F32), 0.0)
        orbital = jnp.sum(orbital, axis=1, keepdims=True).astype(jnp.int32)
        return jnp.sum(jnp.where(orbital == occ_lane, occ[...], 0.0), axis=1, keepdims=True)

    den_buf[...] = vir[...] - (energy(0) + energy(1))
    acc[...] = jnp.zeros_like(acc)

    for step in range(2, 7):
        forward(step)
    pltpu.make_async_copy(amps.at[:, 0:PIECE], a_buf.at[0, 0:ROWS], a_own.at[0]).wait()
    pltpu.make_async_copy(amps.at[:, 0:PIECE], a_buf.at[1, 0:ROWS], a_own.at[1]).wait()
    others = a_buf.at[:, ROWS:512]
    pltpu.make_async_copy(others, others, a_recv).wait()
    own_ints.wait()
    multiply(4, 12)
    twin_copy(0).start()
    forward(7, (0,))
    multiply(3, 11)
    spread(0)
    forward(7, (1,))
    multiply(5, 13)
    twin_copy(1).start()
    forward(7, (2,))
    multiply(2, 14)
    spread(1)
    forward(7, (3,))
    multiply(10, 6)
    twin_copy(2).start()
    forward(8, (0,))
    multiply(1)
    spread(2)
    forward(8, (1,))
    multiply(15)
    finish(0)
    forward(8, (2,))
    multiply(0)
    finish(1)
    forward(8, (3,))
    for at in range(4):
        if at < 2:
            hop(9, 9, at, down).wait_recv()
        else:
            hop(7, 7, at, up).wait_recv()
    multiply(9, 7, lines=slice(256, 512))
    twin_copy(3).start()
    multiply(9, 7, lines=slice(0, 256))
    spread(3)
    finish(2)
    for at in range(4):
        hop(8, 8, at, up).wait_recv()
    multiply(8, lines=slice(256, 512))
    twin_copy(4).start()
    multiply(8, lines=slice(0, 256))
    spread(4)
    finish(3)
    finish(4)
    out[...] = acc[...] / den_buf[...]

    seven = g_buf.at[0, 0:7]
    pltpu.make_async_copy(seven, seven, i_send).wait()
    pltpu.make_async_copy(others, others, a_send).wait()
    for whole, sem in [(g_buf.at[1:Z], r_send), (sib, s_send), (got.at[:, ROWS:256], q_send)]:
        pltpu.make_async_copy(whole, whole, sem).wait()


def per_device(amps, ints, block_of, pair_rows, occ_energy, vir_pair_energy):
    vmem = pl.BlockSpec(memory_space=pltpu.VMEM)
    hbm = pl.BlockSpec(memory_space=pltpu.HBM)
    dma = pltpu.SemaphoreType.DMA
    return pl.pallas_call(
        kernel,
        out_shape=jax.ShapeDtypeStruct((ROWS, 1024), F32),
        in_specs=[hbm, hbm, vmem, vmem, vmem, vmem],
        out_specs=vmem,
        scratch_shapes=[
            pltpu.VMEM((2, 512, PIECE), BF16),
            pltpu.VMEM((Z, 8, ROWS, PIECE), BF16),
            pltpu.VMEM((ROWS, RANGE), BF16),
            pltpu.VMEM((ROWS, CD - TAIL), BF16),
            pltpu.VMEM((ROWS, PIECE), BF16),
            pltpu.VMEM((ROWS, WIDE), BF16),
            pltpu.VMEM((8, 512, LANES), F32),
            pltpu.VMEM((8, 256, LANES), F32),
            pltpu.VMEM((8, 256, LANES), F32),
            pltpu.VMEM((ROWS, 1024), F32),
            pltpu.VMEM((ROWS, 1024), F32),
            dma((2,)), dma, dma((4,)), dma, dma, dma, dma((2,)),
            dma, dma((Z, 4)), dma, dma((5,)), dma, dma((5,)),
        ],
        compiler_params=pltpu.CompilerParams(
            collective_id=0, has_side_effects=True, vmem_limit_bytes=56 * 1024 * 1024
        ),
        cost_estimate=pl.CostEstimate(flops=2700000000, bytes_accessed=4000000, transcendentals=0),
    )(
        amps, ints, block_of.reshape(1, -1), pair_rows.T,
        occ_energy.reshape(1, -1), vir_pair_energy.reshape(1, -1),
    )


def solution(mesh):
    placed = (P(("blk", "pair"), None), P("blk", "pair"), P(), P(("blk", "pair"), None), P(), P())
    return jax.shard_map(
        per_device, mesh=mesh, in_specs=placed, out_specs=P(("blk", "pair"), None), check_vma=False
    )
```

```python
import functools

import jax
import jax.numpy as jnp
from jax import lax
from jax.experimental import pallas as pl
from jax.experimental.pallas import tpu as pltpu
from jax.sharding import PartitionSpec as P

NO = 120
NV = 400
CD = 80200
RANGE = 10025
LANES = 128
WIDE = 10240
PIECE = 1280
LAST_TILE = 547
TAIL = LAST_TILE * LANES + WIDE - PIECE
Z, ZLO, Y, X = 16, 8, 4, 4
PLANE = 32
BLOCKS = 64
ROWS = 16
MESH = pl.DeviceIdType.MESH
F32, BF16 = jnp.float32, jnp.bfloat16

ORDER = (4, 3, 5, 2, 6, 1, 7, 0)
GROUPS = ((0, 1), (1, 3), (3, 5), (5, 7), (7, 8))
FIRST = (0, 1, 2, 3, 4, 5, 14, 15)
FAR = (10, 6, 14, 9, 11, 2, 8, 5, 7, 13, 15, 1, 3, 4, 12)
NEAR = (0, 1, 3, 2)
NT = (((1,), (1,)), ((), ()))


def first_tile(p):
    return jnp.minimum(lax.div(RANGE * p, LANES), LAST_TILE)


def kernel(
    amps, ints, *rest,
):
    small, (out, *scratch) = rest[:4], rest[4:]
    run(amps, ints, small, out, *scratch)


def run(
    amps, ints, small, out, block_of, rows, occ, vir, small_sem,
    a_buf, g_buf, held, last, tail, prep, part, sib, got, acc, den_buf, in_sem,
    i_send, i_recv, i_own, a_send, a_recv, a_own, r_send, r_recv, f_send, s_send, s_recv, q_send, q_recv,
):
    pair, blk = lax.axis_index("pair"), lax.axis_index("blk")
    zh, y = lax.div(pair, Y), lax.rem(pair, Y)
    zl, x, c = lax.div(blk, X * 2), lax.rem(lax.div(blk, 2), X), lax.rem(blk, 2)
    z = zh * ZLO + zl

    def plane(z_at):
        return lax.div(z_at, ZLO) * Y, lax.rem(z_at, ZLO) * (X * 2)

    row, column = plane(z)
    ys, xs = [lax.rem(y + d, Y) for d in range(Y)], [lax.rem(x + d, X) for d in range(X)]
    up, down = plane(lax.rem(z + 1, Z)), plane(lax.rem(z + Z - 1, Z))
    up, down = ((p + y, b + x * 2 + c) for p, b in (up, down))
    twin = (pair, column + x * 2 + 1 - c)

    def device(y_at, x_at, c_at):
        return (row + y_at, column + x_at * 2 + c_at)

    def peer(k):
        dc, dy, dx = lax.div(k, 16), lax.rem(lax.div(k, 4), 4), lax.rem(k, 4)
        return lax.rem(y + dy, Y), lax.rem(x + dx, X), lax.rem(c + dc, 2)

    get_ints = pltpu.make_async_copy(ints, held, in_sem.at[0])
    get_ints.start()
    get_tail = pltpu.make_async_copy(amps.at[:, TAIL:CD], last.at[:, :], in_sem.at[1])
    get_tail.start()

    get_small = [
        pltpu.make_async_copy(src, dst, small_sem.at[i])
        for i, (src, dst) in enumerate(zip(small, (block_of, rows, occ, vir)))
    ]

    barrier = pltpu.get_barrier_semaphore()

    def greet(k, carry):
        pl.semaphore_signal(barrier, inc=1, device_id=device(*peer(k)), device_id_type=MESH)
        return carry

    for where in (up, down):
        pl.semaphore_signal(barrier, inc=1, device_id=where, device_id_type=MESH)
    lax.fori_loop(1, PLANE, greet, 0)

    offset = RANGE * pair - first_tile(pair) * LANES
    shift, skip = lax.rem(offset, LANES), lax.div(offset, LANES)
    lane = lax.broadcasted_iota(jnp.int32, (ROWS, LANES), 1)
    keep = lane >= shift

    def put(tile, value, before):
        now = pltpu.roll(value, shift, 1)
        to = pl.multiple_of(lax.rem(tile + skip, 80) * LANES, LANES)
        prep[:, pl.ds(to, LANES)] = jnp.where(keep, now, before).astype(BF16)
        return now

    def align(i, before):
        for j in range(6):
            tile = i * 6 + j
            at = pl.ds(pl.multiple_of(tile * LANES, LANES), LANES)
            column = RANGE * pair + tile * LANES + lane
            weight = jnp.where(column < NV, 1.0, 2.0)
            before = put(tile, held[:, at].astype(F32) * weight, before)
        return before

    for copy in get_small:
        copy.start()
    get_ints.wait()
    before = lax.fori_loop(0, 13, align, jnp.zeros((ROWS, LANES), F32))
    rest = held[:, 78 * LANES : RANGE].astype(F32) * 2.0
    rest = jnp.concatenate([rest, jnp.zeros((ROWS, 79 * LANES - RANGE), F32)], axis=1)
    before = put(78, rest, before)
    put(79, jnp.zeros((ROWS, LANES), F32), before)
    get_tail.wait()
    tail[:, 0 : PIECE - LANES] = last[:, 0 : PIECE - LANES]
    ending = last[:, PIECE - LANES :]
    tail[:, PIECE - LANES :] = jnp.concatenate([ending, jnp.zeros((ROWS, TAIL + PIECE - CD), BF16)], axis=1)

    pl.semaphore_wait(barrier, PLANE - 1 + 2)

    def ints_copy(x_to, c_to):
        src = prep.at[:, pl.ds(pl.multiple_of((x_to * 2 + c_to) * PIECE, LANES), PIECE)]
        return src, g_buf.at[0, x * 2 + c]

    def send_ints(e, x_to, c_to):
        src, dst = ints_copy(x_to, c_to)
        pltpu.make_async_remote_copy(
            src, dst, i_send, i_recv.at[e], device_id=device(y, x_to, c_to), device_id_type=MESH
        ).start()

    send_ints(0, x, 1 - c)

    def amps_at(half, y_to, x_to, c_to):
        q = x_to * 2 + c_to
        p = half * Y + y_to
        start = pl.multiple_of(first_tile(p) * LANES + q * PIECE, LANES)
        return start, jnp.logical_and(p == 7, q == 7)

    def send_amps(k, carry):
        y_to, x_to, c_to = peer(k)
        for half in range(2):
            start, ends = amps_at(half, y_to, x_to, c_to)
            dst = a_buf.at[half, pl.ds(pl.multiple_of(k * ROWS, ROWS), ROWS)]

            @pl.when(jnp.logical_not(ends))
            def _():
                pltpu.make_async_remote_copy(
                    amps.at[:, pl.ds(start, PIECE)], dst, a_send, a_recv,
                    device_id=device(y_to, x_to, c_to), device_id_type=MESH,
                ).start()

            @pl.when(ends)
            def _():
                pltpu.make_async_remote_copy(
                    tail, dst, a_send, a_recv,
                    device_id=device(y_to, x_to, c_to), device_id_type=MESH,
                ).start()

        return carry

    for half in range(2):
        start, ends = amps_at(half, y, x, c)
        dst = a_buf.at[half, 0:ROWS]

        @pl.when(jnp.logical_not(ends))
        def _():
            pltpu.make_async_copy(amps.at[:, pl.ds(start, PIECE)], dst, a_own.at[half]).start()

        @pl.when(ends)
        def _():
            pltpu.make_async_copy(tail, dst, a_own.at[half]).start()

    def hop(m_from, m_to, at, where):
        sl = pl.ds(xs[-NEAR[at] % X] * 2, 2)
        return pltpu.make_async_remote_copy(
            g_buf.at[m_from, sl], g_buf.at[m_to, sl], r_send, r_recv.at[m_to, at],
            device_id=where, device_id_type=MESH,
        )

    def from_below(z_at):
        return jnp.minimum(lax.div(z_at + 1, 2), 2)

    def last_hops(at):
        sl = pl.ds(xs[-NEAR[at] % X] * 2, 2)
        for side, (m_from, where, wanted) in enumerate((
            (7, up, at < from_below(lax.rem(z + 1, Z))),
            (9, down, at >= from_below(lax.rem(z + Z - 1, Z))),
        )):
            yield wanted, pltpu.make_async_remote_copy(
                g_buf.at[m_from, sl], g_buf.at[8, sl], f_send.at[at, side], r_recv.at[8, at],
                device_id=where, device_id_type=MESH,
            )

    def forward(step, quarters=range(4)):
        for at in quarters:
            ways = [(step, (step - 1) % Z, up), (Z - step, (Z - step + 1) % Z, down)]
            if step == 1 and at == 0:
                continue
            if step == 1:
                came = g_buf.at[0, 0:2]
                pltpu.make_async_copy(came, came, i_recv.at[NEAR[at]]).wait()
            for m_to, m_from, where in ways:
                if step > 1:
                    hop(m_from, m_from, at, where).wait_recv()
                if step < 8:
                    hop(m_from, m_to, at, where).start()
            if step == 8:
                for wanted, copy in last_hops(at):
                    pl.when(wanted)(copy.start)

    def start_ring():
        mine = pltpu.make_async_copy(*ints_copy(x, c), i_own)
        came = g_buf.at[0, 0]
        for own in (True, False):
            at = x * 2 + c if own else x * 2 + 1 - c
            if not own:
                pltpu.make_async_copy(came, came, i_recv.at[0]).wait()
            for m_to, where in ((1, up), (Z - 1, down)):
                pltpu.make_async_remote_copy(
                    ints_copy(x, c)[0] if own else g_buf.at[0, at], g_buf.at[m_to, at],
                    r_send, r_recv.at[m_to, 0], device_id=where, device_id_type=MESH,
                ).start()
            if own:
                mine.start()
                for e in NEAR[1:]:
                    for c_to in (c, 1 - c):
                        send_ints(e, xs[e], c_to)
        return mine

    def multiply(*slots, lines=slice(0, 512)):
        for m in slots:
            o = ORDER.index(m % 8)
            half = lax.div(lax.rem(z + Z - m, Z), ZLO)
            product = lax.dot_general(
                a_buf[half, lines], g_buf[m].reshape(LANES, PIECE), NT, preferred_element_type=F32
            )
            part[o, lines] = product if m in FIRST else part[o, lines] + product

    def twin_copy(group):
        lo, hi = GROUPS[group]
        return pltpu.make_async_remote_copy(
            part.at[lo:hi, 256:512], sib.at[lo:hi], s_send, s_recv.at[group],
            device_id=twin, device_id_type=MESH,
        )

    def spread(group):
        lo, hi = GROUPS[group]
        twin_copy(group).wait_recv()
        for o in range(lo, hi):
            part[o, 0:256] += sib[o]

        for k in FAR:
            sl = slice(k * ROWS, (k + 1) * ROWS)
            pltpu.make_async_remote_copy(
                part.at[lo:hi, sl], got.at[lo:hi, sl], q_send, q_recv.at[group],
                device_id=device(ys[-(k // 4) % Y], xs[-k % X], c), device_id_type=MESH,
            ).start()

    def finish(group):
        lo, hi = GROUPS[group]
        arrived = got.at[lo:hi, ROWS:256]
        pltpu.make_async_copy(arrived, arrived, q_recv.at[group]).wait()
        spot = lax.broadcasted_iota(jnp.int32, (1, LANES), 1)
        for o in range(lo, hi):
            total = part[o, 0:ROWS]
            for k in range(1, 16):
                total = total + got[o, k * ROWS : (k + 1) * ROWS]
            top = total.astype(BF16)
            rest = total - top.astype(F32)
            mid = rest.astype(BF16)
            low = (rest - mid.astype(F32)).astype(BF16)
            block = lax.rem(zl + ZLO - ORDER[o], ZLO)
            rows_at = lax.broadcasted_iota(jnp.int32, (BLOCKS, LANES), 0)
            pick = rows_at == block * 8 + lax.broadcasted_iota(jnp.int32, (BLOCKS, LANES), 1) // 16
            goes = lax.dot_general(
                block_of[...].astype(F32).astype(BF16), jnp.where(pick, 1.0, 0.0).astype(BF16),
                (((1,), (0,)), ((), ())), preferred_element_type=F32,
            )
            goes = goes.astype(jnp.int32) * 16 + spot % 16
            place = lax.broadcasted_iota(jnp.int32, (1024, LANES), 0)
            moves = jnp.where(place == goes, 1.0, 0.0).astype(BF16)
            moved = lax.dot_general(
                jnp.concatenate([top, mid, low], axis=0), moves, NT, preferred_element_type=F32
            )
            acc[...] += moved[0:16] + moved[16:32] + moved[32:48]

    own_ints = start_ring()
    forward(1)
    lax.fori_loop(1, PLANE, send_amps, 0)
    for copy in get_small:
        copy.wait()
    occ_lane = lax.broadcasted_iota(jnp.int32, (ROWS, occ.shape[1]), 1)
    square = (ROWS, ROWS)
    diagonal = lax.broadcasted_iota(jnp.int32, square, 0) == lax.broadcasted_iota(jnp.int32, square, 1)

    def energy(which):
        orbital = jnp.where(diagonal, rows[which : which + 1, :].astype(F32), 0.0)
        orbital = jnp.sum(orbital, axis=1, keepdims=True).astype(jnp.int32)
        return jnp.sum(jnp.where(orbital == occ_lane, occ[...], 0.0), axis=1, keepdims=True)

    den_buf[...] = vir[...] - (energy(0) + energy(1))
    acc[...] = jnp.zeros_like(acc)

    for step in range(2, 7):
        forward(step)
    pltpu.make_async_copy(amps.at[:, 0:PIECE], a_buf.at[0, 0:ROWS], a_own.at[0]).wait()
    pltpu.make_async_copy(amps.at[:, 0:PIECE], a_buf.at[1, 0:ROWS], a_own.at[1]).wait()
    others = a_buf.at[:, ROWS:512]
    pltpu.make_async_copy(others, others, a_recv).wait()
    own_ints.wait()
    multiply(4, 12)
    twin_copy(0).start()
    forward(7, (0,))
    multiply(3, 11)
    spread(0)
    forward(7, (1,))
    multiply(5, 13)
    twin_copy(1).start()
    forward(7, (2,))
    multiply(2, 14)
    spread(1)
    forward(7, (3,))
    multiply(10, 6)
    twin_copy(2).start()
    forward(8, (0,))
    multiply(1)
    spread(2)
    forward(8, (1,))
    multiply(15)
    finish(0)
    forward(8, (2,))
    multiply(0)
    finish(1)
    forward(8, (3,))
    multiply(9, 7, lines=slice(256, 512))
    twin_copy(3).start()
    multiply(9, 7, lines=slice(0, 256))
    spread(3)
    finish(2)
    for at in range(4):
        hop(8, 8, at, up).wait_recv()
    multiply(8, lines=slice(256, 512))
    twin_copy(4).start()
    multiply(8, lines=slice(0, 256))
    spread(4)
    finish(3)
    finish(4)
    out[...] = acc[...] / den_buf[...]

    seven = g_buf.at[0, 0:7]
    pltpu.make_async_copy(seven, seven, i_send).wait()
    pltpu.make_async_copy(others, others, a_send).wait()
    for whole, sem in [(g_buf.at[0 : Z - 2], r_send), (sib, s_send), (got.at[:, ROWS:256], q_send)]:
        pltpu.make_async_copy(whole, whole, sem).wait()
    for at in range(4):
        for wanted, copy in last_hops(at):
            pl.when(wanted)(copy.wait_send)


def per_device(amps, ints, block_of, pair_rows, occ_energy, vir_pair_energy):
    vmem = pl.BlockSpec(memory_space=pltpu.VMEM)
    hbm = pl.BlockSpec(memory_space=pltpu.HBM)
    dma = pltpu.SemaphoreType.DMA
    return pl.pallas_call(
        kernel,
        out_shape=jax.ShapeDtypeStruct((ROWS, 1024), F32),
        in_specs=[hbm] * 6,
        out_specs=vmem,
        scratch_shapes=[
            pltpu.VMEM((1, BLOCKS), jnp.int32), pltpu.VMEM((2, ROWS), jnp.int32),
            pltpu.VMEM((1, NO), F32), pltpu.VMEM((1, 1024), F32), dma((4,)),
            pltpu.VMEM((2, 512, PIECE), BF16),
            pltpu.VMEM((Z, 8, ROWS, PIECE), BF16),
            pltpu.VMEM((ROWS, RANGE), BF16),
            pltpu.VMEM((ROWS, CD - TAIL), BF16),
            pltpu.VMEM((ROWS, PIECE), BF16),
            pltpu.VMEM((ROWS, WIDE), BF16),
            pltpu.VMEM((8, 512, LANES), F32),
            pltpu.VMEM((8, 256, LANES), F32),
            pltpu.VMEM((8, 256, LANES), F32),
            pltpu.VMEM((ROWS, 1024), F32),
            pltpu.VMEM((ROWS, 1024), F32),
            dma((2,)), dma, dma((4,)), dma, dma, dma, dma((2,)),
            dma, dma((Z, 4)), dma((4, 2)), dma, dma((5,)), dma, dma((5,)),
        ],
        compiler_params=pltpu.CompilerParams(
            collective_id=0, has_side_effects=True, vmem_limit_bytes=56 * 1024 * 1024
        ),
        cost_estimate=pl.CostEstimate(flops=2700000000, bytes_accessed=4000000, transcendentals=0),
    )(
        amps, ints, block_of.reshape(1, -1), pair_rows.T,
        occ_energy.reshape(1, -1), vir_pair_energy.reshape(1, -1),
    )


def solution(mesh):
    placed = (P(("blk", "pair"), None), P("blk", "pair"), P(), P(("blk", "pair"), None), P(), P())
    return jax.shard_map(
        per_device, mesh=mesh, in_specs=placed, out_specs=P(("blk", "pair"), None), check_vma=False
    )
```

```python
import functools

import jax
import jax.numpy as jnp
from jax import lax
from jax.experimental import pallas as pl
from jax.experimental.pallas import tpu as pltpu
from jax.sharding import PartitionSpec as P

NO = 120
NV = 400
CD = 80200
RANGE = 10025
LANES = 128
WIDE = 10240
PIECE = 1280
LAST_TILE = 547
TAIL = LAST_TILE * LANES + WIDE - PIECE
Z, ZLO, Y, X = 16, 8, 4, 4
PLANE = 32
BLOCKS = 64
ROWS = 16
MESH = pl.DeviceIdType.MESH
F32, BF16 = jnp.float32, jnp.bfloat16

ORDER = (4, 3, 5, 2, 6, 1, 7, 0)
GROUPS = ((0, 1), (1, 3), (3, 5), (5, 7), (7, 8))
FIRST = (0, 1, 2, 3, 4, 5, 14, 15)
FAR = (10, 6, 14, 9, 11, 2, 8, 5, 7, 13, 15, 1, 3, 4, 12)
NEAR = (0, 1, 3, 2)
NT = (((1,), (1,)), ((), ()))


def first_tile(p):
    return jnp.minimum(lax.div(RANGE * p, LANES), LAST_TILE)


def kernel(
    amps, ints, *rest,
):
    small, (out, *scratch) = rest[:4], rest[4:]
    run(amps, ints, small, out, *scratch)


def run(
    amps, ints, small, out, block_of, rows, occ, vir, small_sem,
    a_buf, g_buf, held, last, tail, prep, part, sib, got, acc, den_buf, in_sem,
    i_send, i_recv, i_own, a_send, a_recv, a_own, r_send, r_recv, f_send, s_send, s_recv, q_send, q_recv,
):
    pair, blk = lax.axis_index("pair"), lax.axis_index("blk")
    zh, y = lax.div(pair, Y), lax.rem(pair, Y)
    zl, x, c = lax.div(blk, X * 2), lax.rem(lax.div(blk, 2), X), lax.rem(blk, 2)
    z = zh * ZLO + zl

    def plane(z_at):
        return lax.div(z_at, ZLO) * Y, lax.rem(z_at, ZLO) * (X * 2)

    row, column = plane(z)
    ys, xs = [lax.rem(y + d, Y) for d in range(Y)], [lax.rem(x + d, X) for d in range(X)]
    up, down = plane(lax.rem(z + 1, Z)), plane(lax.rem(z + Z - 1, Z))
    up, down = ((p + y, b + x * 2 + c) for p, b in (up, down))
    twin = (pair, column + x * 2 + 1 - c)

    def device(y_at, x_at, c_at):
        return (row + y_at, column + x_at * 2 + c_at)

    def peer(k):
        dc, dy, dx = lax.div(k, 16), lax.rem(lax.div(k, 4), 4), lax.rem(k, 4)
        return lax.rem(y + dy, Y), lax.rem(x + dx, X), lax.rem(c + dc, 2)

    get_ints = pltpu.make_async_copy(ints, held, in_sem.at[0])
    get_ints.start()
    get_tail = pltpu.make_async_copy(amps.at[:, TAIL:CD], last.at[:, :], in_sem.at[1])
    get_tail.start()

    get_small = [
        pltpu.make_async_copy(src, dst, small_sem.at[i])
        for i, (src, dst) in enumerate(zip(small, (block_of, rows, occ, vir)))
    ]

    barrier = pltpu.get_barrier_semaphore()

    def greet(k, carry):
        pl.semaphore_signal(barrier, inc=1, device_id=device(*peer(k)), device_id_type=MESH)
        return carry

    for where in (up, down):
        pl.semaphore_signal(barrier, inc=1, device_id=where, device_id_type=MESH)
    lax.fori_loop(1, PLANE, greet, 0)

    offset = RANGE * pair - first_tile(pair) * LANES
    shift, skip = lax.rem(offset, LANES), lax.div(offset, LANES)
    lane = lax.broadcasted_iota(jnp.int32, (ROWS, LANES), 1)
    keep = lane >= shift

    def put(tile, value, before):
        now = pltpu.roll(value, shift, 1)
        to = pl.multiple_of(lax.rem(tile + skip, 80) * LANES, LANES)
        prep[:, pl.ds(to, LANES)] = jnp.where(keep, now, before).astype(BF16)
        return now

    def align(i, before):
        for j in range(6):
            tile = i * 6 + j
            at = pl.ds(pl.multiple_of(tile * LANES, LANES), LANES)
            column = RANGE * pair + tile * LANES + lane
            weight = jnp.where(column < NV, 1.0, 2.0)
            before = put(tile, held[:, at].astype(F32) * weight, before)
        return before

    for copy in get_small:
        copy.start()
    get_ints.wait()
    before = lax.fori_loop(0, 13, align, jnp.zeros((ROWS, LANES), F32))
    rest = held[:, 78 * LANES : RANGE].astype(F32) * 2.0
    rest = jnp.concatenate([rest, jnp.zeros((ROWS, 79 * LANES - RANGE), F32)], axis=1)
    before = put(78, rest, before)
    put(79, jnp.zeros((ROWS, LANES), F32), before)
    get_tail.wait()
    tail[:, 0 : PIECE - LANES] = last[:, 0 : PIECE - LANES]
    ending = last[:, PIECE - LANES :]
    tail[:, PIECE - LANES :] = jnp.concatenate([ending, jnp.zeros((ROWS, TAIL + PIECE - CD), BF16)], axis=1)

    pl.semaphore_wait(barrier, PLANE - 1 + 2)

    def ints_copy(x_to, c_to):
        src = prep.at[:, pl.ds(pl.multiple_of((x_to * 2 + c_to) * PIECE, LANES), PIECE)]
        return src, g_buf.at[0, x * 2 + c]

    def send_ints(e, x_to, c_to):
        src, dst = ints_copy(x_to, c_to)
        pltpu.make_async_remote_copy(
            src, dst, i_send, i_recv.at[e], device_id=device(y, x_to, c_to), device_id_type=MESH
        ).start()

    send_ints(0, x, 1 - c)

    def amps_at(half, y_to, x_to, c_to):
        q = x_to * 2 + c_to
        p = half * Y + y_to
        start = pl.multiple_of(first_tile(p) * LANES + q * PIECE, LANES)
        return start, jnp.logical_and(p == 7, q == 7)

    def send_amps(k, carry):
        y_to, x_to, c_to = peer(k)
        for half in range(2):
            start, ends = amps_at(half, y_to, x_to, c_to)
            dst = a_buf.at[half, pl.ds(pl.multiple_of(k * ROWS, ROWS), ROWS)]

            @pl.when(jnp.logical_not(ends))
            def _():
                pltpu.make_async_remote_copy(
                    amps.at[:, pl.ds(start, PIECE)], dst, a_send, a_recv,
                    device_id=device(y_to, x_to, c_to), device_id_type=MESH,
                ).start()

            @pl.when(ends)
            def _():
                pltpu.make_async_remote_copy(
                    tail, dst, a_send, a_recv,
                    device_id=device(y_to, x_to, c_to), device_id_type=MESH,
                ).start()

        return carry

    for half in range(2):
        start, ends = amps_at(half, y, x, c)
        dst = a_buf.at[half, 0:ROWS]

        @pl.when(jnp.logical_not(ends))
        def _():
            pltpu.make_async_copy(amps.at[:, pl.ds(start, PIECE)], dst, a_own.at[half]).start()

        @pl.when(ends)
        def _():
            pltpu.make_async_copy(tail, dst, a_own.at[half]).start()

    def hop(m_from, m_to, at, where):
        sl = pl.ds(xs[-NEAR[at] % X] * 2, 2)
        return pltpu.make_async_remote_copy(
            g_buf.at[m_from, sl], g_buf.at[m_to, sl], r_send, r_recv.at[m_to, at],
            device_id=where, device_id_type=MESH,
        )

    def from_below(z_at):
        return jnp.minimum(lax.div(z_at, 2), 2)

    def last_hops(at):
        sl = pl.ds(xs[-NEAR[at] % X] * 2, 2)
        for side, (m_from, where, wanted) in enumerate((
            (7, up, at < from_below(lax.rem(z + 1, Z))),
            (9, down, at >= from_below(lax.rem(z + Z - 1, Z))),
        )):
            yield wanted, pltpu.make_async_remote_copy(
                g_buf.at[m_from, sl], g_buf.at[8, sl], f_send.at[at, side], r_recv.at[8, at],
                device_id=where, device_id_type=MESH,
            )

    def forward(step, quarters=range(4)):
        for at in quarters:
            ways = [(step, (step - 1) % Z, up), (Z - step, (Z - step + 1) % Z, down)]
            if step == 1 and at == 0:
                continue
            if step == 1:
                came = g_buf.at[0, 0:2]
                pltpu.make_async_copy(came, came, i_recv.at[NEAR[at]]).wait()
            for m_to, m_from, where in ways:
                if step > 1:
                    hop(m_from, m_from, at, where).wait_recv()
                if step < 8:
                    hop(m_from, m_to, at, where).start()
            if step == 8:
                for wanted, copy in last_hops(at):
                    pl.when(wanted)(copy.start)

    def start_ring():
        mine = pltpu.make_async_copy(*ints_copy(x, c), i_own)
        came = g_buf.at[0, 0]
        for own in (True, False):
            at = x * 2 + c if own else x * 2 + 1 - c
            if not own:
                pltpu.make_async_copy(came, came, i_recv.at[0]).wait()
            for m_to, where in ((1, up), (Z - 1, down)):
                pltpu.make_async_remote_copy(
                    ints_copy(x, c)[0] if own else g_buf.at[0, at], g_buf.at[m_to, at],
                    r_send, r_recv.at[m_to, 0], device_id=where, device_id_type=MESH,
                ).start()
            if own:
                mine.start()
                for e in NEAR[1:]:
                    for c_to in (c, 1 - c):
                        send_ints(e, xs[e], c_to)
        return mine

    def multiply(*slots, lines=slice(0, 512)):
        for m in slots:
            o = ORDER.index(m % 8)
            half = lax.div(lax.rem(z + Z - m, Z), ZLO)
            product = lax.dot_general(
                a_buf[half, lines], g_buf[m].reshape(LANES, PIECE), NT, preferred_element_type=F32
            )
            part[o, lines] = product if m in FIRST else part[o, lines] + product

    def twin_copy(group):
        lo, hi = GROUPS[group]
        return pltpu.make_async_remote_copy(
            part.at[lo:hi, 256:512], sib.at[lo:hi], s_send, s_recv.at[group],
            device_id=twin, device_id_type=MESH,
        )

    def spread(group):
        lo, hi = GROUPS[group]
        twin_copy(group).wait_recv()
        for o in range(lo, hi):
            part[o, 0:256] += sib[o]

        for k in FAR:
            sl = slice(k * ROWS, (k + 1) * ROWS)
            pltpu.make_async_remote_copy(
                part.at[lo:hi, sl], got.at[lo:hi, sl], q_send, q_recv.at[group],
                device_id=device(ys[-(k // 4) % Y], xs[-k % X], c), device_id_type=MESH,
            ).start()

    def finish(group):
        lo, hi = GROUPS[group]
        arrived = got.at[lo:hi, ROWS:256]
        pltpu.make_async_copy(arrived, arrived, q_recv.at[group]).wait()
        spot = lax.broadcasted_iota(jnp.int32, (1, LANES), 1)
        for o in range(lo, hi):
            total = part[o, 0:ROWS]
            for k in range(1, 16):
                total = total + got[o, k * ROWS : (k + 1) * ROWS]
            top = total.astype(BF16)
            rest = total - top.astype(F32)
            mid = rest.astype(BF16)
            low = (rest - mid.astype(F32)).astype(BF16)
            block = lax.rem(zl + ZLO - ORDER[o], ZLO)
            rows_at = lax.broadcasted_iota(jnp.int32, (BLOCKS, LANES), 0)
            pick = rows_at == block * 8 + lax.broadcasted_iota(jnp.int32, (BLOCKS, LANES), 1) // 16
            goes = lax.dot_general(
                block_of[...].astype(F32).astype(BF16), jnp.where(pick, 1.0, 0.0).astype(BF16),
                (((1,), (0,)), ((), ())), preferred_element_type=F32,
            )
            goes = goes.astype(jnp.int32) * 16 + spot % 16
            place = lax.broadcasted_iota(jnp.int32, (1024, LANES), 0)
            moves = jnp.where(place == goes, 1.0, 0.0).astype(BF16)
            moved = lax.dot_general(
                jnp.concatenate([top, mid, low], axis=0), moves, NT, preferred_element_type=F32
            )
            acc[...] += moved[0:16] + moved[16:32] + moved[32:48]

    own_ints = start_ring()
    forward(1, (0, 1, 2))
    lax.fori_loop(1, PLANE, send_amps, 0)
    forward(1, (3,))
    for copy in get_small:
        copy.wait()
    occ_lane = lax.broadcasted_iota(jnp.int32, (ROWS, occ.shape[1]), 1)
    square = (ROWS, ROWS)
    diagonal = lax.broadcasted_iota(jnp.int32, square, 0) == lax.broadcasted_iota(jnp.int32, square, 1)

    def energy(which):
        orbital = jnp.where(diagonal, rows[which : which + 1, :].astype(F32), 0.0)
        orbital = jnp.sum(orbital, axis=1, keepdims=True).astype(jnp.int32)
        return jnp.sum(jnp.where(orbital == occ_lane, occ[...], 0.0), axis=1, keepdims=True)

    den_buf[...] = vir[...] - (energy(0) + energy(1))
    acc[...] = jnp.zeros_like(acc)

    for step in range(2, 7):
        forward(step)
    pltpu.make_async_copy(amps.at[:, 0:PIECE], a_buf.at[0, 0:ROWS], a_own.at[0]).wait()
    pltpu.make_async_copy(amps.at[:, 0:PIECE], a_buf.at[1, 0:ROWS], a_own.at[1]).wait()
    others = a_buf.at[:, ROWS:512]
    pltpu.make_async_copy(others, others, a_recv).wait()
    own_ints.wait()
    multiply(4, 12)
    twin_copy(0).start()
    forward(7, (0,))
    multiply(3, 11)
    spread(0)
    forward(7, (1,))
    multiply(5, 13)
    twin_copy(1).start()
    forward(7, (2,))
    multiply(2, 14)
    spread(1)
    forward(7, (3,))
    multiply(10, 6)
    twin_copy(2).start()
    forward(8, (0,))
    multiply(1)
    spread(2)
    forward(8, (1,))
    multiply(15)
    finish(0)
    forward(8, (2,))
    multiply(0)
    finish(1)
    forward(8, (3,))
    multiply(9, 7, lines=slice(256, 512))
    twin_copy(3).start()
    multiply(9, 7, lines=slice(0, 256))
    spread(3)
    finish(2)
    for at in range(4):
        hop(8, 8, at, up).wait_recv()
    multiply(8, lines=slice(256, 512))
    twin_copy(4).start()
    multiply(8, lines=slice(0, 256))
    spread(4)
    finish(3)
    finish(4)
    out[...] = acc[...] / den_buf[...]

    seven = g_buf.at[0, 0:7]
    pltpu.make_async_copy(seven, seven, i_send).wait()
    pltpu.make_async_copy(others, others, a_send).wait()
    for whole, sem in [(g_buf.at[0 : Z - 2], r_send), (sib, s_send), (got.at[:, ROWS:256], q_send)]:
        pltpu.make_async_copy(whole, whole, sem).wait()
    for at in range(4):
        for wanted, copy in last_hops(at):
            pl.when(wanted)(copy.wait_send)


def per_device(amps, ints, block_of, pair_rows, occ_energy, vir_pair_energy):
    vmem = pl.BlockSpec(memory_space=pltpu.VMEM)
    hbm = pl.BlockSpec(memory_space=pltpu.HBM)
    dma = pltpu.SemaphoreType.DMA
    return pl.pallas_call(
        kernel,
        out_shape=jax.ShapeDtypeStruct((ROWS, 1024), F32),
        in_specs=[hbm] * 6,
        out_specs=vmem,
        scratch_shapes=[
            pltpu.VMEM((1, BLOCKS), jnp.int32), pltpu.VMEM((2, ROWS), jnp.int32),
            pltpu.VMEM((1, NO), F32), pltpu.VMEM((1, 1024), F32), dma((4,)),
            pltpu.VMEM((2, 512, PIECE), BF16),
            pltpu.VMEM((Z, 8, ROWS, PIECE), BF16),
            pltpu.VMEM((ROWS, RANGE), BF16),
            pltpu.VMEM((ROWS, CD - TAIL), BF16),
            pltpu.VMEM((ROWS, PIECE), BF16),
            pltpu.VMEM((ROWS, WIDE), BF16),
            pltpu.VMEM((8, 512, LANES), F32),
            pltpu.VMEM((8, 256, LANES), F32),
            pltpu.VMEM((8, 256, LANES), F32),
            pltpu.VMEM((ROWS, 1024), F32),
            pltpu.VMEM((ROWS, 1024), F32),
            dma((2,)), dma, dma((4,)), dma, dma, dma, dma((2,)),
            dma, dma((Z, 4)), dma((4, 2)), dma, dma((5,)), dma, dma((5,)),
        ],
        compiler_params=pltpu.CompilerParams(
            collective_id=0, has_side_effects=True, vmem_limit_bytes=56 * 1024 * 1024
        ),
        cost_estimate=pl.CostEstimate(flops=2700000000, bytes_accessed=4000000, transcendentals=0),
    )(
        amps, ints, block_of.reshape(1, -1), pair_rows.T,
        occ_energy.reshape(1, -1), vir_pair_energy.reshape(1, -1),
    )


def solution(mesh):
    placed = (P(("blk", "pair"), None), P("blk", "pair"), P(), P(("blk", "pair"), None), P(), P())
    return jax.shard_map(
        per_device, mesh=mesh, in_specs=placed, out_specs=P(("blk", "pair"), None), check_vma=False
    )
```
